512 devices in a mesh: shard: 32 (over z, core), grp: 16 (over y, x).
Axes of the slice: x: 4, y: 4, z: 16, core: 2. Of those that a mesh axis runs over, the one named last changes fastest.
Arguments:
- embeddings: bfloat16 [65536, 4096], P(('shard', 'grp')), parts along dimension 0, as said below
- cluster_ids: int32 [65536], P(('shard', 'grp')), parts along dimension 0, may hold values from 0 to 2047, as said below
- order: int32 [65536], P(('shard', 'grp')), parts along dimension 0, may hold values from 0 to 2047, each once
Outputs:
- best: float32 [65536], P(('shard', 'grp')), parts along dimension 0
The draws below stay inside these ranges and needn't reach their ends.
There are 32 independent parts, one for each index of `shard`. The reference program is written for one: setup_inputs(seed, part) draws one part's arguments, and reference() takes and returns one part's arrays. A program takes and returns all parts, laid end to end along the dimension named above; each array names one. Nothing has to cross between parts.
Inputs may be any that keep to these rules, and one draw needn't show every extreme that they name: `cluster_ids`: never falling along the rows, so each cluster is a run of consecutive rows; a cluster's id is the index of its last row. Exactly one cluster has 1024 rows, every other has 1 to 96. `embeddings`: every row is nonzero.
All inputs are finite; a program needn't handle non-finite values.
Results may differ from the reference program's by a relative error of at most 0.0009.
Values may be sent and summed in bfloat16 or wider, within the bound.
No kernel may reach another device: no remote copies, remote signals or barrier semaphores. Data moves between devices by JAX's collectives and lax.ppermute only.
A program may use at most 64 MiB of HBM per device.

```python
import math
import jax
import jax.numpy as jnp
from jax import lax

D = 4096
ROWS_DEV = 128
TOKENS = 2048
MOST = 1024
SMALL_MOST = 96
N_GRP = 16


def cluster_layout(key):
    key = jax.random.fold_in(key, 11)
    first, second = jax.random.split(key)
    rows = jnp.arange(TOKENS, dtype=jnp.int32)
    begin = jax.random.randint(first, (), 0, TOKENS - MOST + 1)
    inside = (rows >= begin) & (rows < begin + MOST)
    marks = jax.random.randint(second, (TOKENS,), 0, 32) == 0
    forced = (rows - begin) % SMALL_MOST == 0
    starts = jnp.where(inside, rows == begin, marks | forced | (rows == begin + MOST) | (rows == 0))
    next_start = jnp.concatenate([starts[1:], jnp.ones((1,), dtype=bool)])
    ends = jnp.where(next_start, rows, jnp.int32(TOKENS)).astype(jnp.int32)
    return lax.cummin(ends, axis=0, reverse=True).astype(jnp.int32)


def draw_cluster_ids(key, part):
    return cluster_layout(key)


def draw_embeddings(key, part):
    labels = cluster_layout(key)
    key = jax.random.fold_in(key, 5)
    keys = jax.random.split(key, 5)
    centers = jax.random.normal(keys[0], (TOKENS, D), jnp.float32)
    families = jax.random.normal(keys[1], (TOKENS // 8, D), jnp.float32)
    picked = jax.random.randint(keys[2], (TOKENS,), 0, TOKENS // 8)
    scales = jnp.exp(jax.random.uniform(keys[4], (TOKENS, 1), jnp.float32, 0.0, math.log(10.0)))
    noise = 0.5 * jax.random.normal(keys[3], (TOKENS, D), jnp.float32)
    mixed = (0.6 * centers[labels] + families[picked] + noise) * scales
    return mixed.astype(jnp.bfloat16)


def setup_inputs(seed: int = 0, part: int = 0) -> dict:
    key_list = jax.random.split(jax.random.key(seed), 4)
    part_keys = jax.random.split(jax.random.fold_in(key_list[3], part), 4)
    return {
        "embeddings": draw_embeddings(jax.random.fold_in(jax.random.fold_in(key_list[3], part), 71), part),
        "cluster_ids": draw_cluster_ids(jax.random.fold_in(jax.random.fold_in(key_list[3], part), 71), part),
        "order": jax.random.permutation(part_keys[2], TOKENS).astype(jnp.int32),
    }


def reference(embeddings, cluster_ids, order):
    wide = embeddings.astype(jnp.float32)
    squares = lax.optimization_barrier(jnp.sum(wide * wide, axis=1, keepdims=True))
    unit = (wide * lax.rsqrt(squares + 1e-06)).astype(jnp.bfloat16)

    def block(start):
        rows = lax.dynamic_slice_in_dim(unit, start, ROWS_DEV, 0)
        row_ids = lax.dynamic_slice_in_dim(cluster_ids, start, ROWS_DEV, 0)
        row_order = lax.dynamic_slice_in_dim(order, start, ROWS_DEV, 0)
        scores = jnp.dot(rows, unit.T, preferred_element_type=jnp.float32)
        keep = (row_ids[:, None] == cluster_ids[None, :]) & (order[None, :] < row_order[:, None])
        return lax.optimization_barrier(jnp.max(jnp.where(keep, scores, jnp.float32(-1.0)), axis=1))
    starts = (jnp.arange(N_GRP) * ROWS_DEV).astype(jnp.int32)
    return lax.map(block, starts).reshape(TOKENS)
```

```python
import jax
import jax.numpy as jnp
from jax import lax
from jax.experimental import pallas as pl
from jax.experimental.pallas import tpu as pltpu
from jax.sharding import PartitionSpec as P

HALF = 64
EDGE = 96
META = 128
BIG = 1024

FETCH = (
    (3, 8, 14, 15, 7, 1, 11, 4, 9, 5, 6, 10, 0, 12, 13, 2),
    (12, 5, 3, 6, 1, 10, 2, 13, 7, 4, 14, 8, 11, 0, 15, 9),
    (5, 6, 1, 4, 0, 8, 7, 11, 12, 13, 9, 14, 15, 2, 10, 3),
    (15, 13, 10, 2, 6, 4, 5, 3, 11, 14, 12, 7, 1, 9, 0, 8),
)


def dot_nt(left, right):
    return lax.dot_general(left, right, (((1,), (1,)), ((), ())), preferred_element_type=jnp.float32)


def unit_rows(raw):
    wide = raw.astype(jnp.float32)
    squares = jnp.sum(wide * wide, axis=1, keepdims=True)
    return (wide * lax.rsqrt(squares + 1e-06)).astype(jnp.bfloat16)


def pair_form(first, lanes=META):
    a = lax.broadcasted_iota(jnp.int32, (lanes, lanes), 0)
    b = lax.broadcasted_iota(jnp.int32, (lanes, lanes), 1)
    plus = ((a == first) & (b == 2)) | ((a == first + 1) & (b == 3))
    minus = ((a == 2) & (b == first)) | ((a == 3) & (b == first + 1))
    return jnp.where(plus, 1.0, jnp.where(minus, -1.0, 0.0)).astype(jnp.bfloat16)


def difference(meta, first):
    left = jnp.dot(meta, pair_form(first), preferred_element_type=jnp.float32).astype(jnp.bfloat16)
    return dot_nt(left, meta)


def pack_kernel(place, emb, ids, order, msg, edge, meta_out):
    me, core = place[0], place[1]
    width = emb.shape[1]
    rows = emb.shape[0]
    row = lax.broadcasted_iota(jnp.int32, (8, rows), 0)
    lane = lax.broadcasted_iota(jnp.int32, (8, rows), 1)
    id_all = jnp.broadcast_to(ids[...], (8, rows))
    order_all = jnp.broadcast_to(order[...], (8, rows))
    far = jnp.where(id_all - (me * rows + lane) >= EDGE, id_all + 1, 0)
    far = jnp.broadcast_to(jnp.max(far, axis=1, keepdims=True), (8, rows))
    value = jnp.where(row < 2, order_all, jnp.where(row < 6, id_all, far))
    low = value & 127
    parts = jnp.where((row & 1) == 0, value - low, low)
    parts = jnp.where((row == 2) | (row == 3), 1, parts).astype(jnp.float32)
    wide = jnp.concatenate([parts, jnp.zeros((META - 8, rows), jnp.float32)], axis=0)
    meta = wide.T.astype(jnp.bfloat16)
    meta_out[...] = meta
    start = pl.multiple_of(jnp.where(me < 8, HALF, 0), HALF)
    msg[:, :width] = emb[pl.ds(start, HALF), :]
    msg[:, width:] = meta_out[pl.ds(start, HALF), :]
    begin = pl.multiple_of(jnp.where(core == 0, rows - EDGE, 0), 32)
    edge[:, :width] = emb[pl.ds(begin, EDGE), :]
    edge[:, width:] = meta_out[pl.ds(begin, EDGE), :]


def column(meta, first):
    return meta[:, first : first + 1] + meta[:, first + 1 : first + 2]


def merge_kernel(place, own, own_meta, msg, out):
    me = place[0]
    width = own.shape[1]
    rows = 2 * HALF
    is_low = me < 8
    start = pl.multiple_of(jnp.where(is_low, 0, HALF), HALF)
    mine_first = own_meta[0:8, :].astype(jnp.float32)[0:1]
    theirs_first = msg[0:8, width:].astype(jnp.float32)[0:1]
    low_first = jnp.where(is_low, mine_first, theirs_first)
    high_first = jnp.where(is_low, theirs_first, mine_first)
    far = column(low_first, 6)
    last = jnp.where(far > 0, far - 1, column(high_first, 4))
    slot = (me & 7) * rows + jnp.where(is_low, 0, HALF) + lax.broadcasted_iota(jnp.int32, (HALF, 1), 0)
    low_row = (slot.astype(jnp.float32) >= last - (BIG - 1)).astype(jnp.float32)
    take = jnp.where(is_low, low_row, 1.0 - low_row) > 0.5
    raw = jnp.where(take, own[...].astype(jnp.float32), msg[:, :width].astype(jnp.float32))
    squares = jnp.sum(raw * raw, axis=1, keepdims=True)
    out[:, :width] = (raw * lax.rsqrt(squares + 1e-06)).astype(jnp.bfloat16)
    mine = own_meta[pl.ds(start, HALF), :].astype(jnp.float32)
    meta = jnp.where(take, mine, msg[:, width:].astype(jnp.float32))
    lane = lax.broadcasted_iota(jnp.int32, (HALF, META), 1)
    high = jnp.floor(last * (1.0 / 128)) * 128
    meta = jnp.where(lane == 6, high, jnp.where(lane == 7, last - high, meta))
    out[:, width:] = meta.astype(jnp.bfloat16)


def near_kernel(emb, own_meta, edge, msg, best, unit, meta):
    width = emb.shape[1]
    rows = emb.shape[0]
    for ref, begin, count in ((emb, 0, rows), (edge, rows, EDGE), (msg, rows + EDGE, HALF)):
        for at in range(0, count, 32):
            unit[begin + at : begin + at + 32, :] = unit_rows(ref[at : at + 32, :width])
    meta[0:rows, :] = own_meta[...]
    meta[rows : rows + EDGE, :] = edge[:, width:]
    meta[rows + EDGE :, :] = msg[:, width:]
    total = rows + EDGE + HALF
    scores = dot_nt(unit[...], unit[...])
    keep = (difference(meta[...], 4) == 0) & (difference(meta[...], 0) < 0)
    found = jnp.max(jnp.where(keep, scores, -1.0), axis=0, keepdims=True)
    best[...] = jnp.broadcast_to(found, (8, total))


def far_kernel(place, *refs):
    blocks, metas, (near, out, scores) = refs[:5], refs[5:10], refs[10:]
    step = pl.program_id(0)
    rows = 2 * HALF
    part = jnp.concatenate([b[...] for b in blocks], axis=0)
    product = dot_nt(part, part)

    @pl.when(step == 0)
    def _():
        scores[...] = product

    @pl.when(step > 0)
    def _():
        scores[...] += product

    @pl.when(step == pl.num_programs(0) - 1)
    def _():
        me, core = place[0], place[1]
        meta = jnp.concatenate([m[...] for m in metas], axis=0)
        keep = difference(meta, 0) < 0
        found = jnp.max(jnp.where(keep, scores[...], -1.0), axis=0, keepdims=True)
        dest = lax.broadcasted_iota(jnp.int32, (16, rows), 0)
        lane = lax.broadcasted_iota(jnp.int32, (16, rows), 1)
        last = column(metas[0][0:8, :].astype(jnp.float32)[0:1], 6).astype(jnp.int32)
        at = dest * rows + lane
        inside = (at <= last) & (at > last - BIG)
        total = jnp.full((16, rows), -1.0, jnp.float32)
        for k in range(5):
            group = place[2 + k]
            piece = found[:, k * HALF : (k + 1) * HALF]
            both = jnp.concatenate([piece, piece], axis=1)
            here = inside & ((dest & 7) == (group & 7)) & ((lane >= HALF) == (group >= 8))
            total = jnp.maximum(total, jnp.where(here, both, -1.0))
        none = jnp.full((1, rows - EDGE), -1.0, jnp.float32)
        own = near[0:1, 0:rows]
        side = near[0:1, rows : rows + EDGE]
        other = near[0:1, rows + EDGE :]
        total = jnp.maximum(total, jnp.where(dest == me, own, -1.0))
        before = jnp.concatenate([none, side], axis=1)
        after = jnp.concatenate([side, none], axis=1)
        total = jnp.maximum(total, jnp.where((core == 0) & (dest == ((me + 15) & 15)), before, -1.0))
        total = jnp.maximum(total, jnp.where((core == 1) & (dest == ((me + 1) & 15)), after, -1.0))
        there = (dest == (me ^ 8)) & ((lane >= HALF) == (me >= 8))
        total = jnp.maximum(total, jnp.where(there, jnp.concatenate([other, other], axis=1), -1.0))
        out[...] = total


def solution(mesh):
    n_shard, n_grp = mesh.shape["shard"], mesh.shape["grp"]
    axes = ("shard", "grp")

    def swap(pairs_of):
        return [(s * n_grp + a, s * n_grp + b) for s in range(n_shard) for a, b in pairs_of(s % 2)]

    partner = swap(lambda core: [(p, p ^ 8) for p in range(n_grp)])
    edges = swap(lambda core: [(p, (p + 1 - 2 * core) % n_grp) for p in range(n_grp)])
    fetch = [swap(lambda core: [(f[t], t) for t in range(n_grp)]) for f in FETCH]
    smem = pl.BlockSpec(memory_space=pltpu.SMEM)
    vmem = pl.BlockSpec(memory_space=pltpu.VMEM)

    def body(embeddings, cluster_ids, order):
        rows, width = embeddings.shape
        bf16, f32 = jnp.bfloat16, jnp.float32
        me = lax.axis_index("grp")
        core = lax.axis_index("shard") & 1
        table = jnp.array([[t] + [f[t] for f in FETCH] for t in range(n_grp)], jnp.int32)
        place = jnp.concatenate([jnp.stack([me, core]), table[me]]).astype(jnp.int32)
        msg, edge, meta = pl.pallas_call(
            pack_kernel,
            out_shape=(
                jax.ShapeDtypeStruct((HALF, width + META), bf16),
                jax.ShapeDtypeStruct((EDGE, width + META), bf16),
                jax.ShapeDtypeStruct((rows, META), bf16),
            ),
            in_specs=[smem, vmem, vmem, vmem],
            out_specs=(vmem, vmem, vmem),
            compiler_params=pltpu.CompilerParams(vmem_limit_bytes=32 << 20),
            name="pack",
        )(place, embeddings, cluster_ids.reshape(1, rows), order.reshape(1, rows))
        msg = lax.ppermute(msg, axes, partner)
        edge = lax.ppermute(edge, axes, edges)
        mine = pl.pallas_call(
            merge_kernel,
            grid_spec=pltpu.PrefetchScalarGridSpec(
                num_scalar_prefetch=1,
                grid=(1,),
                in_specs=[
                    pl.BlockSpec((HALF, width), lambda i, place: (place[0] // 8, 0)),
                    pl.BlockSpec((rows, META), lambda i, place: (0, 0)),
                    pl.BlockSpec((HALF, width + META), lambda i, place: (0, 0)),
                ],
                out_specs=pl.BlockSpec((HALF, width + META), lambda i, place: (0, 0)),
            ),
            out_shape=jax.ShapeDtypeStruct((HALF, width + META), bf16),
            compiler_params=pltpu.CompilerParams(vmem_limit_bytes=32 << 20),
            name="merge",
        )(place, embeddings, meta, msg)
        got = [lax.ppermute(mine, axes, f) for f in fetch]
        total = rows + EDGE + HALF
        near = pl.pallas_call(
            near_kernel,
            out_shape=jax.ShapeDtypeStruct((8, total), f32),
            in_specs=[vmem] * 4,
            out_specs=vmem,
            scratch_shapes=[pltpu.VMEM((total, width), bf16), pltpu.VMEM((total, META), bf16)],
            compiler_params=pltpu.CompilerParams(vmem_limit_bytes=32 << 20),
            cost_estimate=pl.CostEstimate(flops=2 * total * total * width, bytes_accessed=2 * total * width, transcendentals=0),
            name="near",
        )(embeddings, meta, edge, msg)
        blocks = [mine] + got
        chunk = min(1024, width)
        table = pl.pallas_call(
            far_kernel,
            grid_spec=pltpu.PrefetchScalarGridSpec(
                num_scalar_prefetch=1,
                grid=(width // chunk,),
                in_specs=[pl.BlockSpec((HALF, chunk), lambda i, place: (0, i))] * 5
                + [pl.BlockSpec((HALF, META), lambda i, place: (0, width // META))] * 5
                + [pl.BlockSpec((8, total), lambda i, place: (0, 0))],
                out_specs=pl.BlockSpec((16, rows), lambda i, place: (0, 0)),
                scratch_shapes=[pltpu.VMEM((5 * HALF, 5 * HALF), f32)],
            ),
            out_shape=jax.ShapeDtypeStruct((16, rows), f32),
            compiler_params=pltpu.CompilerParams(vmem_limit_bytes=32 << 20),
            name="far",
        )(place, *blocks, *blocks, near)
        table = lax.all_to_all(table, "grp", 0, 0, tiled=True)
        return jnp.max(table, axis=0)

    return jax.shard_map(
        body,
        mesh=mesh,
        in_specs=(P(axes, None), P(axes), P(axes)),
        out_specs=P(axes),
        check_vma=False,
    )
```

```python
import functools

import jax
import jax.numpy as jnp
from jax import lax
from jax.experimental import pallas as pl
from jax.experimental.pallas import tpu as pltpu
from jax.sharding import PartitionSpec as P

META = 128

FETCH = (
    (
        (0, 5, 1, 2, 6, 4, 10, 3, 9, 12, 14, 7, 13, 8, 15, 11),
        (0, 13, 3, 7, 8, 1, 2, 5, 4, 9, 11, 10, 12, 14, 6, 15),
        (8, 0, 1, 4, 12, 7, 5, 6, 11, 10, 3, 15, 14, 2, 9, 13),
        (1, 6, 15, 0, 5, 9, 4, 11, 3, 13, 10, 8, 7, 14, 2, 12),
    ),
    (
        (1, 2, 8, 12, 7, 11, 4, 3, 13, 5, 6, 10, 14, 9, 15, 0),
        (12, 5, 2, 7, 4, 6, 9, 8, 11, 10, 14, 15, 0, 1, 13, 3),
        (3, 1, 0, 10, 5, 12, 2, 6, 4, 8, 13, 9, 15, 14, 7, 11),
        (4, 13, 6, 2, 0, 5, 10, 1, 9, 3, 11, 7, 8, 12, 14, 15),
    ),
)
COUNT = len(FETCH[0])


def dot_nt(left, right):
    return lax.dot_general(left, right, (((1,), (1,)), ((), ())), preferred_element_type=jnp.float32)


def pair_form(first):
    a = lax.broadcasted_iota(jnp.int32, (META, META), 0)
    b = lax.broadcasted_iota(jnp.int32, (META, META), 1)
    plus = ((a == first) & (b == 2)) | ((a == first + 1) & (b == 3))
    minus = ((a == 2) & (b == first)) | ((a == 3) & (b == first + 1))
    return jnp.where(plus, 1.0, jnp.where(minus, -1.0, 0.0)).astype(jnp.bfloat16)


def difference(left, right, first):
    turned = jnp.dot(left, pair_form(first), preferred_element_type=jnp.float32)
    return dot_nt(turned.astype(jnp.bfloat16), right)


def pack_kernel(emb, ids, order, msg):
    rows, width = emb.shape
    row = lax.broadcasted_iota(jnp.int32, (8, rows), 0)
    value = jnp.where(row < 2, jnp.broadcast_to(order[...], (8, rows)), jnp.broadcast_to(ids[...], (8, rows)))
    low = value & 127
    parts = jnp.where((row & 1) == 0, value - low, low)
    parts = jnp.where((row == 2) | (row == 3), 1, parts)
    parts = jnp.where(row < 6, parts, 0).astype(jnp.float32)
    wide = jnp.concatenate([parts, jnp.zeros((META - 8, rows), jnp.float32)], axis=0)
    msg[:, width:] = wide.T.astype(jnp.bfloat16)
    for at in range(0, rows, 32):
        block = emb[at : at + 32, :].astype(jnp.float32)
        squares = jnp.sum(block * block, axis=1, keepdims=True)
        msg[at : at + 32, :width] = (block * lax.rsqrt(squares + 1e-06)).astype(jnp.bfloat16)


def meet(olds, new, scores):
    rows = new.shape[0]
    width = new.shape[1] - META
    blocks = [*olds, new]
    chunk = min(1024, width)
    for at in range(0, width, chunk):
        part = jnp.concatenate([b[:, at : at + chunk] for b in blocks], axis=0)
        product = dot_nt(new[:, at : at + chunk], part)
        if at == 0:
            scores[...] = product
        else:
            scores[...] += product
    meta = jnp.concatenate([b[:, width:] for b in blocks], axis=0)
    mine = new[:, width:]
    ahead = difference(mine, meta, 0)
    same = difference(mine, meta, 4) == 0
    value = scores[...]
    down = jnp.max(jnp.where(same & (ahead < 0), value, -1.0), axis=0, keepdims=True)
    across = jnp.where(same & (ahead > 0), value, -1.0)
    most = functools.reduce(jnp.maximum, [across[:, k * rows : (k + 1) * rows] for k in range(len(blocks))])
    turned = jnp.max(most.T, axis=0, keepdims=True)
    return down, turned


def meet_kernel(count, *refs):
    olds, new, before, out, scores = refs[:count], refs[count], refs[count + 1 : -2], refs[-2], refs[-1]
    rows = new.shape[0]
    down, turned = meet(olds, new, scores)
    if before:
        down = jnp.maximum(down, jnp.concatenate([before[0][0:1], turned], axis=1))
    else:
        down = jnp.maximum(down, turned)
    out[...] = jnp.broadcast_to(down, out.shape)


def last_kernel(count, table, *refs):
    olds, new, before, out, scores = refs[:count], refs[count], refs[count + 1], refs[-2], refs[-1]
    rows = new.shape[0]
    down, turned = meet(olds, new, scores)
    down = jnp.maximum(down, jnp.concatenate([before[0:1], turned], axis=1))
    me = lax.axis_index("grp")
    place = (lax.axis_index("shard") & 1) * 16 + me
    dest = lax.broadcasted_iota(jnp.int32, (16, rows), 0)
    total = jnp.where(dest == me, down[:, :rows], -1.0)
    for k in range(count):
        piece = down[:, (k + 1) * rows : (k + 2) * rows]
        total = jnp.maximum(total, jnp.where(dest == table[place, k], piece, -1.0))
    out[...] = total


def solution(mesh):
    n_shard, n_grp = mesh.shape["shard"], mesh.shape["grp"]
    axes = ("shard", "grp")

    def pairs(k):
        return [
            (s * n_grp + FETCH[s % 2][k][t], s * n_grp + t)
            for s in range(n_shard)
            for t in range(n_grp)
            if FETCH[s % 2][k][t] != t
        ]

    smem = pl.BlockSpec(memory_space=pltpu.SMEM)
    vmem = pl.BlockSpec(memory_space=pltpu.VMEM)
    params = pltpu.CompilerParams(vmem_limit_bytes=32 << 20)

    def body(embeddings, cluster_ids, order):
        rows, width = embeddings.shape
        f32 = jnp.float32
        mine = pl.pallas_call(
            pack_kernel,
            out_shape=jax.ShapeDtypeStruct((rows, width + META), jnp.bfloat16),
            in_specs=[vmem] * 3,
            out_specs=vmem,
            compiler_params=params,
            name="pack",
        )(embeddings, cluster_ids.reshape(1, rows), order.reshape(1, rows))
        blocks = [mine] + [lax.ppermute(mine, axes, pairs(k)) for k in range(COUNT)]
        table = jnp.array([[f[k][t] for k in range(COUNT)] for f in FETCH for t in range(n_grp)], jnp.int32)
        best = []
        for count in range(COUNT + 1):
            total = (count + 1) * rows
            last = count == COUNT
            kernel = functools.partial(last_kernel if last else meet_kernel, count)
            out = (n_grp, rows) if last else (8, total)
            best = [
                pl.pallas_call(
                    kernel,
                    out_shape=jax.ShapeDtypeStruct(out, f32),
                    in_specs=[smem] * last + [vmem] * (count + 1 + len(best)),
                    out_specs=vmem,
                    scratch_shapes=[pltpu.VMEM((rows, total), f32)],
                    compiler_params=params,
                    cost_estimate=pl.CostEstimate(flops=2 * rows * total * width, bytes_accessed=2 * total * width, transcendentals=0),
                    name="meet_%d" % count,
                )(*([table] if last else []), *blocks[: count + 1], *best)
            ]
        given = lax.all_to_all(best[0], "grp", 0, 0, tiled=True)
        return jnp.max(given, axis=0)

    return jax.shard_map(
        body,
        mesh=mesh,
        in_specs=(P(axes, None), P(axes), P(axes)),
        out_specs=P(axes),
        check_vma=False,
    )
```

```python
import functools

import jax
import jax.numpy as jnp
from jax import lax
from jax.experimental import pallas as pl
from jax.experimental.pallas import tpu as pltpu
from jax.sharding import PartitionSpec as P

META = 128

ROUTE = (
    (
        (4, 2, 1, 0, 7, 6, 5, 3, 12, 10, 11, 8, 15, 9, 13, 14),
        (12, 5, 14, 15, 0, 4, 7, 11, 9, 8, 6, 10, 13, 1, 2, 3),
        (1, 0, 3, 2, 8, 4, 7, 11, 12, 5, 6, 15, 13, 9, 10, 14),
        (12, 5, 6, 0, 7, 9, 2, 3, 4, 10, 14, 8, 15, 1, 13, 11),
        (2, 0, 0, 0, 2, 2, 1, 1, 2, 2, 0, 2, 2, 1, 2, 1),
        (1, 2, 2, 2, 1, 1, 2, 2, 1, 2, 2, 1, 0, 1, 1, 2),
    ),
    (
        (1, 0, 3, 2, 5, 9, 10, 6, 4, 13, 14, 7, 8, 12, 15, 11),
        (3, 13, 6, 7, 8, 1, 2, 4, 11, 5, 9, 15, 0, 14, 10, 12),
        (3, 2, 1, 7, 0, 6, 5, 4, 9, 13, 11, 10, 8, 14, 15, 12),
        (4, 13, 14, 15, 5, 1, 10, 6, 11, 8, 9, 7, 0, 12, 2, 3),
        (2, 0, 2, 2, 2, 0, 2, 2, 1, 1, 2, 1, 1, 1, 2, 1),
        (1, 1, 1, 1, 1, 1, 1, 1, 2, 1, 1, 2, 1, 1, 2, 2),
    ),
)


def dot_nt(left, right):
    return lax.dot_general(left, right, (((1,), (1,)), ((), ())), preferred_element_type=jnp.float32)


def key_difference(left, right):
    a = lax.broadcasted_iota(jnp.int32, (META, META), 0)
    b = lax.broadcasted_iota(jnp.int32, (META, META), 1)
    plus = (b == a + 2) & ((a & 2) == 0)
    minus = (a == b + 2) & ((b & 2) == 0)
    size = jnp.where(a < 4, 1.0, jnp.where(a < 8, 4096.0, 0.0))
    form = jnp.where(plus, size, jnp.where(minus, -size, 0.0)).astype(jnp.bfloat16)
    turned = jnp.dot(left, form, preferred_element_type=jnp.float32)
    return dot_nt(turned.astype(jnp.bfloat16), right)


def pack_kernel(emb, numbers, *outs):
    rows, width = emb.shape
    row = lax.broadcasted_iota(jnp.int32, (16, rows), 0)
    value = jnp.where(row < 4, jnp.broadcast_to(numbers[1:2], (16, rows)), jnp.broadcast_to(numbers[0:1], (16, rows)))
    low = value & 127
    parts = jnp.where((row & 2) == 2, 1, jnp.where((row & 1) == 0, value - low, low))
    parts = jnp.where(row < 8, parts, lax.axis_index("grp")).astype(jnp.float32)
    wide = jnp.concatenate([parts, jnp.zeros((META - 16, rows), jnp.float32)], axis=0)
    meta = wide.T.astype(jnp.bfloat16)
    half = rows // 2
    for i, out in enumerate(outs):
        out[:, width:] = meta[i * half : (i + 1) * half]
        for at in range(0, half, 32):
            block = emb[i * half + at : i * half + at + 32, :].astype(jnp.float32)
            squares = jnp.sum(block * block, axis=1, keepdims=True)
            out[at : at + 32, :width] = (block * lax.rsqrt(squares + 1e-06)).astype(jnp.bfloat16)


def meet(blocks, count):
    width = blocks[0].shape[1] - META
    every = jnp.concatenate([b[:, :width] for b in blocks], axis=0)
    every_meta = jnp.concatenate([b[:, width:] for b in blocks], axis=0)
    new = jnp.concatenate([b[:, :width] for b in blocks[-count:]], axis=0)
    new_meta = jnp.concatenate([b[:, width:] for b in blocks[-count:]], axis=0)
    ahead = key_difference(new_meta, every_meta)
    scores = dot_nt(new, every)
    down = jnp.max(jnp.where((ahead < 0) & (ahead > -2048), scores, -1.0), axis=0, keepdims=True)
    if count == len(blocks):
        return down
    across = jnp.where((ahead > 0) & (ahead < 2048), scores, -1.0)
    lanes = new.shape[0]
    most = functools.reduce(jnp.maximum, [across[:, at : at + lanes] for at in range(0, across.shape[1], lanes)])
    turned = jnp.max(most.T, axis=0, keepdims=True)
    rest = jnp.full((1, down.shape[1] - lanes), -1.0, jnp.float32)
    return jnp.maximum(down, jnp.concatenate([rest, turned], axis=1))


def meet_kernel(number, count, *refs):
    blocks, before, out = refs[:number], refs[number:-1], refs[-1]
    best = meet(blocks, count)
    if before:
        old = before[0].shape[1]
        best = jnp.concatenate([jnp.maximum(best[:, :old], before[0][0:1]), best[:, old:]], axis=1)
    out[...] = jnp.broadcast_to(best, out.shape)


def last_kernel(number, count, *refs):
    blocks, before, out = refs[:number], refs[number], refs[-1]
    half, width = blocks[0].shape[0], blocks[0].shape[1] - META
    best = meet(blocks, count)
    old = before.shape[1]
    best = jnp.concatenate([jnp.maximum(best[:, :old], before[0:1]), best[:, old:]], axis=1)
    parts = [best[:, k * half : (k + 1) * half] for k in range(number)]
    dest = lax.broadcasted_iota(jnp.int32, (16, 2 * half), 0).astype(jnp.float32)
    total = jnp.full((16, 2 * half), -1.0, jnp.float32)
    for low, high in ((0, 1), (2, 3), (4, 5), (6, 8), (7, 9)):
        device = blocks[low][0:16, width:].astype(jnp.float32)[0:1, 8:9]
        value = jnp.concatenate([parts[low], parts[high]], axis=1)
        total = jnp.maximum(total, jnp.where(dest == device, value, -1.0))
    out[...] = total


def my_place():
    return (lax.axis_index("shard") & 1) * 16 + lax.axis_index("grp")


def signed(bits):
    return bits - (1 << 32) if bits >> 31 else bits


def choose_kernel(own, first, second, *outs):
    place = my_place()
    for j, out in enumerate(outs):
        for k, ref in enumerate((own, first, second)):
            users = sum(1 << (16 * c + t) for c in range(2) for t in range(16) if ROUTE[c][4 + j][t] == k)

            @pl.when(((jnp.int32(signed(users)) >> place) & 1) == 1)
            def _(ref=ref, out=out):
                out[...] = ref[...]


def solution(mesh):
    n_shard, n_grp = mesh.shape["shard"], mesh.shape["grp"]
    axes = ("shard", "grp")

    def pairs(k):
        return [(s * n_grp + ROUTE[s % 2][k][t], s * n_grp + t) for s in range(n_shard) for t in range(n_grp)]

    vmem = pl.BlockSpec(memory_space=pltpu.VMEM)
    params = pltpu.CompilerParams(vmem_limit_bytes=32 << 20)

    def body(embeddings, cluster_ids, order):
        rows, width = embeddings.shape
        half = rows // 2
        f32 = jnp.float32
        piece = jax.ShapeDtypeStruct((half, width + META), jnp.bfloat16)

        def meet_call(kernel, count, out, blocks, *before):
            flops = 2 * len(blocks) * count * half * half * width
            return pl.pallas_call(
                functools.partial(kernel, len(blocks), count),
                out_shape=jax.ShapeDtypeStruct(out, f32),
                in_specs=[vmem] * (len(blocks) + len(before)),
                out_specs=vmem,
                compiler_params=params,
                cost_estimate=pl.CostEstimate(flops=flops, bytes_accessed=2 * len(blocks) * half * width, transcendentals=0),
                name=kernel.__name__,
            )(*blocks, *before)

        own = pl.pallas_call(
            pack_kernel,
            out_shape=(piece, piece),
            in_specs=[vmem] * 2,
            out_specs=(vmem, vmem),
            compiler_params=params,
            name="pack",
        )(embeddings, jnp.stack([cluster_ids, order]))
        got = [[lax.ppermute(own[i], axes, pairs(k)) for k in (0, 1)] for i in (0, 1)]
        came = []
        for i in (0, 1):
            passed = pl.pallas_call(
                choose_kernel,
                out_shape=(piece, piece),
                in_specs=[vmem] * 3,
                out_specs=(vmem, vmem),
                compiler_params=params,
                name="choose",
            )(own[i], *got[i])
            came.append([lax.ppermute(passed[k], axes, pairs(2 + k)) for k in (0, 1)])
        near = [own[0], own[1], got[0][0], got[1][0], got[0][1], got[1][1]]
        best = meet_call(meet_kernel, 6, (8, 6 * half), near)
        best = meet_call(meet_kernel, 2, (8, 8 * half), near + came[0], best)
        table = meet_call(last_kernel, 2, (n_grp, rows), near + came[0] + came[1], best)
        given = lax.all_to_all(table, "grp", 0, 0, tiled=True)
        return jnp.max(given, axis=0)

    return jax.shard_map(
        body,
        mesh=mesh,
        in_specs=(P(axes, None), P(axes), P(axes)),
        out_specs=P(axes),
        check_vma=False,
    )
```

```python
import functools

import jax
import jax.numpy as jnp
from jax import lax
from jax.experimental import pallas as pl
from jax.experimental.pallas import tpu as pltpu
from jax.sharding import PartitionSpec as P

META = 128

ROUTE = (
    (
        (1, 0, 3, 2, 5, 9, 10, 6, 4, 13, 14, 7, 8, 12, 15, 11),
        (3, 13, 6, 7, 8, 1, 2, 4, 11, 5, 9, 15, 0, 14, 10, 12),
        (3, 2, 1, 7, 0, 6, 5, 4, 9, 13, 11, 10, 8, 14, 15, 12),
        (4, 13, 14, 15, 5, 1, 10, 6, 11, 8, 9, 7, 0, 12, 2, 3),
        (2, 0, 2, 2, 2, 0, 2, 2, 1, 1, 2, 1, 1, 1, 2, 1),
        (1, 1, 1, 1, 1, 1, 1, 1, 2, 1, 1, 2, 1, 1, 2, 2),
    ),
    (
        (4, 2, 1, 0, 7, 6, 5, 3, 12, 10, 11, 8, 15, 9, 13, 14),
        (12, 5, 14, 15, 0, 4, 7, 11, 9, 8, 6, 10, 13, 1, 2, 3),
        (1, 0, 3, 2, 8, 4, 7, 11, 12, 5, 6, 15, 13, 9, 10, 14),
        (12, 5, 6, 0, 7, 9, 2, 3, 4, 10, 14, 8, 15, 1, 13, 11),
        (2, 0, 0, 0, 2, 2, 1, 1, 2, 2, 0, 2, 2, 1, 2, 1),
        (1, 2, 2, 2, 1, 1, 2, 2, 1, 2, 2, 1, 0, 1, 1, 2),
    ),
)


def dot_nt(left, right):
    return lax.dot_general(left, right, (((1,), (1,)), ((), ())), preferred_element_type=jnp.float32)


def key_difference(left, right):
    a = lax.broadcasted_iota(jnp.int32, (META, META), 0)
    b = lax.broadcasted_iota(jnp.int32, (META, META), 1)
    plus = (b == a + 2) & ((a & 2) == 0)
    minus = (a == b + 2) & ((b & 2) == 0)
    size = jnp.where(a < 4, 1.0, jnp.where(a < 8, 4096.0, 0.0))
    form = jnp.where(plus, size, jnp.where(minus, -size, 0.0)).astype(jnp.bfloat16)
    turned = jnp.dot(left, form, preferred_element_type=jnp.float32)
    return dot_nt(turned.astype(jnp.bfloat16), right)


def pack_kernel(emb, numbers, *outs):
    rows, width = emb.shape
    row = lax.broadcasted_iota(jnp.int32, (16, rows), 0)
    value = jnp.where(row < 4, jnp.broadcast_to(numbers[1:2], (16, rows)), jnp.broadcast_to(numbers[0:1], (16, rows)))
    low = value & 127
    parts = jnp.where((row & 2) == 2, 1, jnp.where((row & 1) == 0, value - low, low))
    parts = jnp.where(row < 8, parts, lax.axis_index("grp")).astype(jnp.float32)
    wide = jnp.concatenate([parts, jnp.zeros((META - 16, rows), jnp.float32)], axis=0)
    meta = wide.T.astype(jnp.bfloat16)
    half = rows // 2
    for i, out in enumerate(outs):
        out[:, width:] = meta[i * half : (i + 1) * half]
        for at in range(0, half, 32):
            block = emb[i * half + at : i * half + at + 32, :].astype(jnp.float32)
            squares = jnp.sum(block * block, axis=1, keepdims=True)
            out[at : at + 32, :width] = (block * lax.rsqrt(squares + 1e-06)).astype(jnp.bfloat16)


def meet(blocks, count):
    width = blocks[0].shape[1] - META
    every = jnp.concatenate([b[:, :width] for b in blocks], axis=0)
    every_meta = jnp.concatenate([b[:, width:] for b in blocks], axis=0)
    new = jnp.concatenate([b[:, :width] for b in blocks[-count:]], axis=0)
    new_meta = jnp.concatenate([b[:, width:] for b in blocks[-count:]], axis=0)
    ahead = key_difference(new_meta, every_meta)
    scores = dot_nt(new, every)
    down = jnp.max(jnp.where((ahead < 0) & (ahead > -2048), scores, -1.0), axis=0, keepdims=True)
    if count == len(blocks):
        return down
    across = jnp.where((ahead > 0) & (ahead < 2048), scores, -1.0)
    lanes = new.shape[0]
    most = functools.reduce(jnp.maximum, [across[:, at : at + lanes] for at in range(0, across.shape[1], lanes)])
    turned = jnp.max(most.T, axis=0, keepdims=True)
    rest = jnp.full((1, down.shape[1] - lanes), -1.0, jnp.float32)
    return jnp.maximum(down, jnp.concatenate([rest, turned], axis=1))


def meet_kernel(number, count, *refs):
    blocks, before, out = refs[:number], refs[number:-1], refs[-1]
    best = meet(blocks, count)
    if before:
        old = before[0].shape[1]
        best = jnp.concatenate([jnp.maximum(best[:, :old], before[0][0:1]), best[:, old:]], axis=1)
    out[...] = jnp.broadcast_to(best, out.shape)


def last_kernel(number, count, *refs):
    blocks, before, out = refs[:number], refs[number], refs[-1]
    half, width = blocks[0].shape[0], blocks[0].shape[1] - META
    best = meet(blocks, count)
    old = before.shape[1]
    best = jnp.concatenate([jnp.maximum(best[:, :old], before[0:1]), best[:, old:]], axis=1)
    parts = [best[:, k * half : (k + 1) * half] for k in range(number)]
    dest = lax.broadcasted_iota(jnp.int32, (16, 2 * half), 0).astype(jnp.float32)
    total = jnp.full((16, 2 * half), -1.0, jnp.float32)
    for low, high in ((0, 1), (2, 3), (4, 5), (6, 8), (7, 9)):
        device = blocks[low][0:16, width:].astype(jnp.float32)[0:1, 8:9]
        value = jnp.concatenate([parts[low], parts[high]], axis=1)
        total = jnp.maximum(total, jnp.where(dest == device, value, -1.0))
    out[...] = total


def my_place():
    return (lax.axis_index("shard") & 1) * 16 + lax.axis_index("grp")


def signed(bits):
    return bits - (1 << 32) if bits >> 31 else bits


def choose_kernel(own, first, second, *outs):
    place = my_place()
    for j, out in enumerate(outs):
        for k, ref in enumerate((own, first, second)):
            users = sum(1 << (16 * c + t) for c in range(2) for t in range(16) if ROUTE[c][4 + j][t] == k)

            @pl.when(((jnp.int32(signed(users)) >> place) & 1) == 1)
            def _(ref=ref, out=out):
                out[...] = ref[...]


def solution(mesh):
    n_shard, n_grp = mesh.shape["shard"], mesh.shape["grp"]
    axes = ("shard", "grp")

    def pairs(k):
        return [(s * n_grp + ROUTE[s % 2][k][t], s * n_grp + t) for s in range(n_shard) for t in range(n_grp)]

    vmem = pl.BlockSpec(memory_space=pltpu.VMEM)
    params = pltpu.CompilerParams(vmem_limit_bytes=32 << 20)

    def body(embeddings, cluster_ids, order):
        rows, width = embeddings.shape
        half = rows // 2
        f32 = jnp.float32
        piece = jax.ShapeDtypeStruct((half, width + META), jnp.bfloat16)

        def meet_call(kernel, count, out, blocks, *before):
            flops = 2 * len(blocks) * count * half * half * width
            return pl.pallas_call(
                functools.partial(kernel, len(blocks), count),
                out_shape=jax.ShapeDtypeStruct(out, f32),
                in_specs=[vmem] * (len(blocks) + len(before)),
                out_specs=vmem,
                compiler_params=params,
                cost_estimate=pl.CostEstimate(flops=flops, bytes_accessed=2 * len(blocks) * half * width, transcendentals=0),
                name=kernel.__name__,
            )(*blocks, *before)

        own = pl.pallas_call(
            pack_kernel,
            out_shape=(piece, piece),
            in_specs=[vmem] * 2,
            out_specs=(vmem, vmem),
            compiler_params=params,
            name="pack",
        )(embeddings, jnp.stack([cluster_ids, order]))
        got = [[lax.ppermute(own[i], axes, pairs(k)) for k in (0, 1)] for i in (0, 1)]
        came = []
        for i in (0, 1):
            passed = pl.pallas_call(
                choose_kernel,
                out_shape=(piece, piece),
                in_specs=[vmem] * 3,
                out_specs=(vmem, vmem),
                compiler_params=params,
                name="choose",
            )(own[i], *got[i])
            came.append([lax.ppermute(passed[k], axes, pairs(2 + k)) for k in (0, 1)])
        near = [own[0], own[1], got[0][0], got[1][0], got[0][1], got[1][1]]
        best = meet_call(meet_kernel, 6, (8, 6 * half), near)
        best = meet_call(meet_kernel, 2, (8, 8 * half), near + came[0], best)
        table = meet_call(last_kernel, 2, (n_grp, rows), near + came[0] + came[1], best)
        given = lax.all_to_all(table, "grp", 0, 0, tiled=True)
        return jnp.max(given, axis=0)

    return jax.shard_map(
        body,
        mesh=mesh,
        in_specs=(P(axes, None), P(axes), P(axes)),
        out_specs=P(axes),
        check_vma=False,
    )
```

```python
import functools

import jax
import jax.numpy as jnp
from jax import lax
from jax.experimental import pallas as pl
from jax.experimental.pallas import tpu as pltpu
from jax.sharding import PartitionSpec as P

META = 128

ROUTE = (
    (
        (4, 5, 3, 7, 0, 1, 2, 11, 9, 13, 6, 10, 8, 12, 15, 14),
        (3, 0, 1, 15, 8, 6, 10, 4, 11, 5, 14, 7, 13, 9, 2, 12),
        (3, 13, 1, 15, 8, 6, 7, 4, 11, 5, 9, 10, 0, 14, 2, 12),
        (12, 0, 3, 7, 5, 4, 2, 6, 9, 10, 14, 15, 8, 1, 13, 11),
        (2, 1, 1, 1, 1, 1, 1, 2, 1, 1, 1, 2, 1, 1, 0, 1),
        (1, 1, 1, 1, 2, 2, 1, 1, 2, 2, 0, 1, 2, 2, 1, 2),
    ),
    (
        (12, 2, 14, 0, 7, 9, 5, 6, 4, 10, 11, 8, 15, 1, 13, 3),
        (1, 13, 6, 2, 5, 4, 7, 3, 12, 8, 9, 15, 0, 14, 10, 11),
        (1, 2, 14, 0, 7, 9, 5, 11, 4, 13, 6, 8, 15, 12, 10, 3),
        (4, 5, 6, 2, 0, 1, 10, 3, 12, 8, 11, 7, 13, 9, 15, 14),
        (1, 2, 2, 0, 2, 1, 2, 2, 1, 1, 2, 1, 0, 1, 2, 2),
        (2, 1, 2, 2, 1, 0, 2, 1, 2, 2, 1, 2, 2, 0, 0, 1),
    ),
)


def dot_nt(left, right):
    return lax.dot_general(left, right, (((1,), (1,)), ((), ())), preferred_element_type=jnp.float32)


def key_difference(left, right):
    a = lax.broadcasted_iota(jnp.int32, (META, META), 0)
    b = lax.broadcasted_iota(jnp.int32, (META, META), 1)
    plus = (b == a + 2) & ((a & 2) == 0)
    minus = (a == b + 2) & ((b & 2) == 0)
    size = jnp.where(a < 4, 1.0, jnp.where(a < 8, 4096.0, 0.0))
    form = jnp.where(plus, size, jnp.where(minus, -size, 0.0)).astype(jnp.bfloat16)
    turned = jnp.dot(left, form, preferred_element_type=jnp.float32)
    return dot_nt(turned.astype(jnp.bfloat16), right)


def pack_kernel(emb, numbers, *outs):
    rows, width = emb.shape
    row = lax.broadcasted_iota(jnp.int32, (16, rows), 0)
    value = jnp.where(row < 4, jnp.broadcast_to(numbers[1:2], (16, rows)), jnp.broadcast_to(numbers[0:1], (16, rows)))
    low = value & 127
    parts = jnp.where((row & 2) == 2, 1, jnp.where((row & 1) == 0, value - low, low))
    parts = jnp.where(row < 8, parts, lax.axis_index("grp")).astype(jnp.float32)
    wide = jnp.concatenate([parts, jnp.zeros((META - 16, rows), jnp.float32)], axis=0)
    meta = wide.T.astype(jnp.bfloat16)
    half = rows // 2
    for i, out in enumerate(outs):
        out[:, width:] = meta[i * half : (i + 1) * half]
        for at in range(0, half, 32):
            block = emb[i * half + at : i * half + at + 32, :].astype(jnp.float32)
            squares = jnp.sum(block * block, axis=1, keepdims=True)
            out[at : at + 32, :width] = (block * lax.rsqrt(squares + 1e-06)).astype(jnp.bfloat16)


def meet(blocks, count):
    width = blocks[0].shape[1] - META
    every = jnp.concatenate([b[:, :width] for b in blocks], axis=0)
    every_meta = jnp.concatenate([b[:, width:] for b in blocks], axis=0)
    new = jnp.concatenate([b[:, :width] for b in blocks[-count:]], axis=0)
    new_meta = jnp.concatenate([b[:, width:] for b in blocks[-count:]], axis=0)
    ahead = key_difference(new_meta, every_meta)
    scores = dot_nt(new, every)
    down = jnp.max(jnp.where((ahead < 0) & (ahead > -2048), scores, -1.0), axis=0, keepdims=True)
    if count == len(blocks):
        return down
    across = jnp.where((ahead > 0) & (ahead < 2048), scores, -1.0)
    lanes = new.shape[0]
    most = functools.reduce(jnp.maximum, [across[:, at : at + lanes] for at in range(0, across.shape[1], lanes)])
    turned = jnp.max(most.T, axis=0, keepdims=True)
    rest = jnp.full((1, down.shape[1] - lanes), -1.0, jnp.float32)
    return jnp.maximum(down, jnp.concatenate([rest, turned], axis=1))


def meet_kernel(number, count, *refs):
    blocks, before, out = refs[:number], refs[number:-1], refs[-1]
    best = meet(blocks, count)
    if before:
        old = before[0].shape[1]
        best = jnp.concatenate([jnp.maximum(best[:, :old], before[0][0:1]), best[:, old:]], axis=1)
    out[...] = jnp.broadcast_to(best, out.shape)


def last_kernel(number, count, *refs):
    blocks, before, out = refs[:number], refs[number], refs[-1]
    half, width = blocks[0].shape[0], blocks[0].shape[1] - META
    best = meet(blocks, count)
    old = before.shape[1]
    best = jnp.concatenate([jnp.maximum(best[:, :old], before[0:1]), best[:, old:]], axis=1)
    parts = [best[:, k * half : (k + 1) * half] for k in range(number)]
    dest = lax.broadcasted_iota(jnp.int32, (16, 2 * half), 0).astype(jnp.float32)
    total = jnp.full((16, 2 * half), -1.0, jnp.float32)
    for low, high in ((0, 1), (2, 3), (4, 5), (6, 8), (7, 9)):
        device = blocks[low][0:16, width:].astype(jnp.float32)[0:1, 8:9]
        value = jnp.concatenate([parts[low], parts[high]], axis=1)
        total = jnp.maximum(total, jnp.where(dest == device, value, -1.0))
    out[...] = total


def my_place():
    return (lax.axis_index("shard") & 1) * 16 + lax.axis_index("grp")


def signed(bits):
    return bits - (1 << 32) if bits >> 31 else bits


def choose_kernel(own, first, second, *outs):
    place = my_place()
    for j, out in enumerate(outs):
        for k, ref in enumerate((own, first, second)):
            users = sum(1 << (16 * c + t) for c in range(2) for t in range(16) if ROUTE[c][4 + j][t] == k)

            @pl.when(((jnp.int32(signed(users)) >> place) & 1) == 1)
            def _(ref=ref, out=out):
                out[...] = ref[...]


def solution(mesh):
    n_shard, n_grp = mesh.shape["shard"], mesh.shape["grp"]
    axes = ("shard", "grp")

    def pairs(k):
        return [(s * n_grp + ROUTE[s % 2][k][t], s * n_grp + t) for s in range(n_shard) for t in range(n_grp)]

    vmem = pl.BlockSpec(memory_space=pltpu.VMEM)
    params = pltpu.CompilerParams(vmem_limit_bytes=32 << 20)

    def body(embeddings, cluster_ids, order):
        rows, width = embeddings.shape
        half = rows // 2
        f32 = jnp.float32
        piece = jax.ShapeDtypeStruct((half, width + META), jnp.bfloat16)

        def meet_call(kernel, count, out, blocks, *before):
            flops = 2 * len(blocks) * count * half * half * width
            return pl.pallas_call(
                functools.partial(kernel, len(blocks), count),
                out_shape=jax.ShapeDtypeStruct(out, f32),
                in_specs=[vmem] * (len(blocks) + len(before)),
                out_specs=vmem,
                compiler_params=params,
                cost_estimate=pl.CostEstimate(flops=flops, bytes_accessed=2 * len(blocks) * half * width, transcendentals=0),
                name=kernel.__name__,
            )(*blocks, *before)

        own = pl.pallas_call(
            pack_kernel,
            out_shape=(piece, piece),
            in_specs=[vmem] * 2,
            out_specs=(vmem, vmem),
            compiler_params=params,
            name="pack",
        )(embeddings, jnp.stack([cluster_ids, order]))
        got = [[lax.ppermute(own[i], axes, pairs(k)) for k in (0, 1)] for i in (0, 1)]
        came = []
        for i in (0, 1):
            passed = pl.pallas_call(
                choose_kernel,
                out_shape=(piece, piece),
                in_specs=[vmem] * 3,
                out_specs=(vmem, vmem),
                compiler_params=params,
                name="choose",
            )(own[i], *got[i])
            came.append([lax.ppermute(passed[k], axes, pairs(2 + k)) for k in (0, 1)])
        near = [own[0], own[1], got[0][0], got[1][0], got[0][1], got[1][1]]
        best = meet_call(meet_kernel, 6, (8, 6 * half), near)
        best = meet_call(meet_kernel, 2, (8, 8 * half), near + came[0], best)
        table = meet_call(last_kernel, 2, (n_grp, rows), near + came[0] + came[1], best)
        given = lax.all_to_all(table, "grp", 0, 0, tiled=True)
        return jnp.max(given, axis=0)

    return jax.shard_map(
        body,
        mesh=mesh,
        in_specs=(P(axes, None), P(axes), P(axes)),
        out_specs=P(axes),
        check_vma=False,
    )
```

```python
import functools

import jax
import jax.numpy as jnp
from jax import lax
from jax.experimental import pallas as pl
from jax.experimental.pallas import tpu as pltpu
from jax.sharding import PartitionSpec as P

META = 128
FIRST = 80

ROUTE = (
    (
        (4, 5, 3, 7, 0, 1, 2, 11, 9, 13, 6, 10, 8, 12, 15, 14),
        (3, 0, 1, 15, 8, 6, 10, 4, 11, 5, 14, 7, 13, 9, 2, 12),
        (3, 13, 1, 15, 8, 6, 7, 4, 11, 5, 9, 10, 0, 14, 2, 12),
        (12, 0, 3, 7, 5, 4, 2, 6, 9, 10, 14, 15, 8, 1, 13, 11),
        (2, 1, 1, 1, 1, 1, 1, 2, 1, 1, 1, 2, 1, 1, 0, 1),
        (1, 1, 1, 1, 2, 2, 1, 1, 2, 2, 0, 1, 2, 2, 1, 2),
    ),
    (
        (12, 2, 14, 0, 7, 9, 5, 6, 4, 10, 11, 8, 15, 1, 13, 3),
        (1, 13, 6, 2, 5, 4, 7, 3, 12, 8, 9, 15, 0, 14, 10, 11),
        (1, 2, 14, 0, 7, 9, 5, 11, 4, 13, 6, 8, 15, 12, 10, 3),
        (4, 5, 6, 2, 0, 1, 10, 3, 12, 8, 11, 7, 13, 9, 15, 14),
        (1, 2, 2, 0, 2, 1, 2, 2, 1, 1, 2, 1, 0, 1, 2, 2),
        (2, 1, 2, 2, 1, 0, 2, 1, 2, 2, 1, 2, 2, 0, 0, 1),
    ),
)


def dot_nt(left, right):
    return lax.dot_general(left, right, (((1,), (1,)), ((), ())), preferred_element_type=jnp.float32)


def key_difference(left, right):
    a = lax.broadcasted_iota(jnp.int32, (META, META), 0)
    b = lax.broadcasted_iota(jnp.int32, (META, META), 1)
    plus = (b == a + 2) & ((a & 2) == 0)
    minus = (a == b + 2) & ((b & 2) == 0)
    size = jnp.where(a < 4, 1.0, jnp.where(a < 8, 4096.0, 0.0))
    form = jnp.where(plus, size, jnp.where(minus, -size, 0.0)).astype(jnp.bfloat16)
    turned = jnp.dot(left, form, preferred_element_type=jnp.float32)
    return dot_nt(turned.astype(jnp.bfloat16), right)


def pack_kernel(emb, numbers, *outs):
    rows, width = emb.shape
    row = lax.broadcasted_iota(jnp.int32, (16, rows), 0)
    value = jnp.where(row < 4, jnp.broadcast_to(numbers[1:2], (16, rows)), jnp.broadcast_to(numbers[0:1], (16, rows)))
    low = value & 127
    parts = jnp.where((row & 2) == 2, 1, jnp.where((row & 1) == 0, value - low, low))
    parts = jnp.where(row < 8, parts, lax.axis_index("grp")).astype(jnp.float32)
    wide = jnp.concatenate([parts, jnp.zeros((META - 16, rows), jnp.float32)], axis=0)
    meta = wide.T.astype(jnp.bfloat16)
    begin = 0
    for out in outs:
        count = out.shape[0]
        out[:, width:] = meta[begin : begin + count]
        for at in range(0, count, 16):
            block = emb[begin + at : begin + at + 16, :].astype(jnp.float32)
            squares = jnp.sum(block * block, axis=1, keepdims=True)
            out[at : at + 16, :width] = (block * lax.rsqrt(squares + 1e-06)).astype(jnp.bfloat16)
        begin += count


def meet(blocks, count):
    width = blocks[0].shape[1] - META
    every = jnp.concatenate([b[:, :width] for b in blocks], axis=0)
    every_meta = jnp.concatenate([b[:, width:] for b in blocks], axis=0)
    new = jnp.concatenate([b[:, :width] for b in blocks[-count:]], axis=0)
    new_meta = jnp.concatenate([b[:, width:] for b in blocks[-count:]], axis=0)
    ahead = key_difference(new_meta, every_meta)
    scores = dot_nt(new, every)
    down = jnp.max(jnp.where((ahead < 0) & (ahead > -2048), scores, -1.0), axis=0, keepdims=True)
    if count == len(blocks):
        return down
    across = jnp.where((ahead > 0) & (ahead < 2048), scores, -1.0)
    lanes = new.shape[0]
    most = jnp.max(across, axis=1, keepdims=True)
    turned = jnp.broadcast_to(most, (lanes, 128)).T[0:1]
    rest = jnp.full((1, down.shape[1] - lanes), -1.0, jnp.float32)
    return jnp.maximum(down, jnp.concatenate([rest, turned], axis=1))


def meet_kernel(number, count, *refs):
    blocks, before, out = refs[:number], refs[number:-1], refs[-1]
    best = meet(blocks, count)
    if before:
        old = before[0].shape[1]
        best = jnp.concatenate([jnp.maximum(best[:, :old], before[0][0:1]), best[:, old:]], axis=1)
    out[...] = jnp.broadcast_to(best, out.shape)


def last_kernel(number, count, *refs):
    blocks, before, out = refs[:number], refs[number], refs[-1]
    rows, width = blocks[0].shape[0] + blocks[1].shape[0], blocks[0].shape[1] - META
    best = meet(blocks, count)
    old = before.shape[1]
    best = jnp.concatenate([jnp.maximum(best[:, :old], before[0:1]), best[:, old:]], axis=1)
    ends = [sum(b.shape[0] for b in blocks[: k + 1]) for k in range(number)]
    parts = [best[:, end - b.shape[0] : end] for end, b in zip(ends, blocks)]
    dest = lax.broadcasted_iota(jnp.int32, (16, rows), 0).astype(jnp.float32)
    total = jnp.full((16, rows), -1.0, jnp.float32)
    for low, high in ((0, 1), (2, 3), (4, 5), (6, 8), (7, 9)):
        device = blocks[low][0:16, width:].astype(jnp.float32)[0:1, 8:9]
        value = jnp.concatenate([parts[low], parts[high]], axis=1)
        total = jnp.maximum(total, jnp.where(dest == device, value, -1.0))
    out[...] = total


def my_place():
    return (lax.axis_index("shard") & 1) * 16 + lax.axis_index("grp")


def signed(bits):
    return bits - (1 << 32) if bits >> 31 else bits


def choose_kernel(own, first, second, *outs):
    place = my_place()
    for j, out in enumerate(outs):
        for k, ref in enumerate((own, first, second)):
            users = sum(1 << (16 * c + t) for c in range(2) for t in range(16) if ROUTE[c][4 + j][t] == k)

            @pl.when(((jnp.int32(signed(users)) >> place) & 1) == 1)
            def _(ref=ref, out=out):
                out[...] = ref[...]


def solution(mesh):
    n_shard, n_grp = mesh.shape["shard"], mesh.shape["grp"]
    axes = ("shard", "grp")

    def pairs(k):
        return [(s * n_grp + ROUTE[s % 2][k][t], s * n_grp + t) for s in range(n_shard) for t in range(n_grp)]

    vmem = pl.BlockSpec(memory_space=pltpu.VMEM)
    params = pltpu.CompilerParams(vmem_limit_bytes=32 << 20)

    def body(embeddings, cluster_ids, order):
        rows, width = embeddings.shape
        f32 = jnp.float32
        pieces = [jax.ShapeDtypeStruct((n, width + META), jnp.bfloat16) for n in (FIRST, rows - FIRST)]

        def meet_call(kernel, count, blocks, *before):
            total, new = (sum(b.shape[0] for b in bs) for bs in (blocks, blocks[-count:]))
            out = (n_grp, rows) if kernel is last_kernel else (8, total)
            return pl.pallas_call(
                functools.partial(kernel, len(blocks), count),
                out_shape=jax.ShapeDtypeStruct(out, f32),
                in_specs=[vmem] * (len(blocks) + len(before)),
                out_specs=vmem,
                compiler_params=params,
                cost_estimate=pl.CostEstimate(flops=2 * total * new * width, bytes_accessed=2 * total * width, transcendentals=0),
                name=kernel.__name__,
            )(*blocks, *before)

        own = pl.pallas_call(
            pack_kernel,
            out_shape=tuple(pieces),
            in_specs=[vmem] * 2,
            out_specs=(vmem, vmem),
            compiler_params=params,
            name="pack",
        )(embeddings, jnp.stack([cluster_ids, order]))
        got = [[lax.ppermute(own[i], axes, pairs(k)) for k in (0, 1)] for i in (0, 1)]
        came = []
        for i in (0, 1):
            passed = pl.pallas_call(
                choose_kernel,
                out_shape=(pieces[i], pieces[i]),
                in_specs=[vmem] * 3,
                out_specs=(vmem, vmem),
                compiler_params=params,
                name="choose",
            )(own[i], *got[i])
            came.append([lax.ppermute(passed[k], axes, pairs(2 + k)) for k in (0, 1)])
        near = [own[0], own[1], got[0][0], got[1][0], got[0][1], got[1][1]]
        best = meet_call(meet_kernel, 6, near)
        best = meet_call(meet_kernel, 2, near + came[0], best)
        table = meet_call(last_kernel, 2, near + came[0] + came[1], best)
        given = lax.all_to_all(table, "grp", 0, 0, tiled=True)
        return jnp.max(given, axis=0)

    return jax.shard_map(
        body,
        mesh=mesh,
        in_specs=(P(axes, None), P(axes), P(axes)),
        out_specs=P(axes),
        check_vma=False,
    )
```
